512 devices in a mesh: dp: 64 (over y, x, z_hi, core), tensor: 8 (over z_lo).
Axes of the slice: x: 4, y: 4, z: 16 (z_hi: 2, z_lo: 8; z = z_hi * 8 + z_lo), core: 2. Of those that a mesh axis runs over, the one named last changes fastest.
Arguments:
- trainer_key_inputs: bfloat16 [131072, 4096], P('dp', 'tensor'), may hold values from -6 to 6
- cotangent: bfloat16 [131072, 512], P('dp', 'tensor'), may hold values from -6 to 6
- adapter_down_factor: float32 [4096, 64], P('tensor'), may hold values from -0.09375 to 0.09375
- adapter_up_factor: float32 [64, 512], P(None, 'tensor'), may hold values from -0.75 to 0.75
- frozen_key_weight: bfloat16 [4096, 512], P('tensor'), may hold values from -0.09375 to 0.09375
- hidden: bfloat16 [16384, 4, 4096], P('dp', None, 'tensor'), may hold values from -6 to 6
- positions: int32 [16384], P(('dp', 'tensor')), may hold values from 0 to 4091
- key_norm_gain: float32 [128], replicated, may hold values from 0.5 to 1.5
Outputs:
- keys: bfloat16 [16384, 4, 512], P(('dp', 'tensor'))
- updated_down_factor: float32 [4096, 64], P('tensor')
- updated_up_factor: float32 [64, 512], P(None, 'tensor')
The draws below stay inside these ranges and needn't reach their ends.
All inputs are finite; a program needn't handle non-finite values.
Results may differ from the reference program's by a relative error of at most 0.009.
Values may be sent and summed in bfloat16 or wider, within the bound.
No kernel may reach another device: no remote copies, remote signals or barrier semaphores. Data moves between devices by JAX's collectives and lax.ppermute only.
A program may use at most 64 MiB of HBM per device.

```python
import jax
import jax.numpy as jnp
from jax import lax

MODEL_WIDTH = 4096
HEAD_DIM = 128
KV_HEADS = 4
ADAPTER_RANK = 64
STEPS = 4
POSITIONS = 4096
ROWS = 256
KEY_WIDTH = 512
TOKENS = 131072
ALL_ROWS = 16384
N_DP = 64


def with_ends(drawn, key, smallest, high):
    shape = drawn.shape
    place = [jax.random.randint(jax.random.fold_in(key, axis), (), 0, shape[axis]) for axis in range(len(shape))]
    drawn = drawn.at[tuple(place)].set(smallest)
    longest = shape.index(max(shape))
    place[longest] = (place[longest] + 1) % shape[longest]
    return drawn.at[tuple(place)].set(high)


def levels(rng, dims, shards, low, top_value):
    def one(axis_at, shards_of):
        steps = jax.random.uniform(jax.random.fold_in(jax.random.fold_in(rng, 6), axis_at), (shards_of,), jnp.float32, low / len(shards), top_value / len(shards))
        return jnp.repeat(jnp.exp(steps), dims[axis_at] // shards_of).reshape((-1,) + (1,) * (len(dims) - axis_at - 1))

    factor_of = one(*shards[0])
    for cut in shards[1:]:
        factor_of = factor_of * one(*cut)
    return factor_of


def centred(stream_key, shape, scale, reach, pieces=(), kind=jnp.bfloat16):
    drawn = scale * jax.random.normal(stream_key, shape, jnp.float32)
    if pieces:
        drawn = drawn * levels(stream_key, shape, pieces, -0.22, 0.18)
    return jnp.clip(drawn, -reach, reach).astype(kind)


def setup_inputs(seed: int = 0) -> dict:
    key_of = jax.random.split(jax.random.key(seed), 9)
    return {
        "trainer_key_inputs": centred(key_of[0], (TOKENS, MODEL_WIDTH), 1.0, 6.0, ((0, 64), (1, 8))),
        "cotangent": centred(key_of[1], (TOKENS, KEY_WIDTH), 1.0, 6.0, ((0, 64), (1, 8))),
        "adapter_down_factor": centred(key_of[2], (MODEL_WIDTH, ADAPTER_RANK), MODEL_WIDTH ** -0.5, 0.09375, ((0, 8),), jnp.float32),
        "adapter_up_factor": centred(key_of[3], (ADAPTER_RANK, KEY_WIDTH), ADAPTER_RANK ** -0.5, 0.75, ((1, 8),), jnp.float32),
        "frozen_key_weight": centred(key_of[4], (MODEL_WIDTH, KEY_WIDTH), MODEL_WIDTH ** -0.5, 0.09375, ((0, 8),)),
        "hidden": centred(key_of[5], (ALL_ROWS, STEPS, MODEL_WIDTH), 1.0, 6.0, ((0, 64), (2, 8))),
        "positions": with_ends(jax.random.randint(key_of[6], (ALL_ROWS,), 0, POSITIONS - STEPS), jax.random.fold_in(key_of[6], 1), 0, (POSITIONS - STEPS) - 1).astype(jnp.int32),
        "key_norm_gain": jnp.clip(1.0 + 0.1 * jax.random.normal(key_of[7], (HEAD_DIM,), jnp.float32), 0.5, 1.5),
    }


adapter_scale = 2.0
step_length = 8.0
epsilon = 1e-06
theta_base = 1000000.0

def rotate(normed, starts):
    half = HEAD_DIM // 2
    index = jnp.arange(half, dtype=jnp.float32)
    freqs = jnp.exp(-jnp.log(jnp.float32(theta_base)) * 2.0 * index / HEAD_DIM)
    places = (starts[:, None] + jnp.arange(STEPS, dtype=jnp.int32)[None, :]).astype(jnp.float32)
    angle = places[:, :, None, None] * freqs[None, None, None, :]
    cosine = jnp.cos(angle)
    sine = jnp.sin(angle)
    first = normed[..., :half]
    second = normed[..., half:]
    return jnp.concatenate([first * cosine - second * sine, second * cosine + first * sine], axis=-1)

def reference(trainer_key_inputs, cotangent, adapter_down_factor, adapter_up_factor, frozen_key_weight, hidden, positions, key_norm_gain):
    down_factor_slice = adapter_down_factor.astype(jnp.bfloat16)
    up_factor_slice = adapter_up_factor.astype(jnp.bfloat16)
    down_activation = jnp.dot(trainer_key_inputs, down_factor_slice, preferred_element_type=jnp.float32).astype(jnp.bfloat16)
    backward_activation = jnp.dot(cotangent, up_factor_slice.T, preferred_element_type=jnp.float32).astype(jnp.bfloat16)
    down_gradient = adapter_scale * jnp.dot(trainer_key_inputs.T, backward_activation, preferred_element_type=jnp.float32)
    up_gradient = adapter_scale * jnp.dot(down_activation.T, cotangent, preferred_element_type=jnp.float32)
    total = jnp.sum(down_gradient * down_gradient) + jnp.sum(up_gradient * up_gradient)
    factor_matrix = step_length / jnp.sqrt(total + epsilon)
    updated_down_factor = adapter_down_factor - factor_matrix * down_gradient
    updated_up_factor = adapter_up_factor - factor_matrix * up_gradient
    a_new_low = updated_down_factor.astype(jnp.bfloat16)
    up_factor_expanded = updated_up_factor.astype(jnp.bfloat16).astype(jnp.float32)

    def engine(args):
        states, starts = args
        flat = states.reshape(ROWS * STEPS, MODEL_WIDTH)
        frozen_output = jnp.dot(flat, frozen_key_weight, preferred_element_type=jnp.float32)
        rank_activation = jnp.dot(flat, a_new_low, preferred_element_type=jnp.float32)
        key_projection = frozen_output + adapter_scale * jnp.dot(rank_activation, up_factor_expanded, precision=lax.Precision.HIGHEST, preferred_element_type=jnp.float32)
        heads = key_projection.reshape(ROWS, STEPS, KV_HEADS, HEAD_DIM)
        normed = heads * lax.rsqrt(lax.optimization_barrier(jnp.mean(heads * heads, axis=-1, keepdims=True)) + epsilon) * key_norm_gain
        return rotate(normed, starts).reshape(ROWS, STEPS, KEY_WIDTH).astype(jnp.bfloat16)
    keys = lax.map(engine, (hidden.reshape(N_DP, ROWS, STEPS, MODEL_WIDTH), positions.reshape(N_DP, ROWS)))
    return (keys.reshape(N_DP * ROWS, STEPS, KEY_WIDTH), updated_down_factor, updated_up_factor)
```

```python
import jax
import jax.numpy as jnp
from jax import lax
from jax.sharding import Mesh
from jax.sharding import PartitionSpec as P

HEAD_DIM = 128
KV_HEADS = 4
STEPS = 4

adapter_scale = 2.0
step_length = 8.0
epsilon = 1e-06
theta_base = 1000000.0

TENSOR = ("t2", "t1", "t0")
PLANE = ("y", "x", "core")
SWAP = [(0, 1), (1, 0)]
bf16 = jnp.bfloat16
f32 = jnp.float32


def rotate(normed, starts):
    half = HEAD_DIM // 2
    index = jnp.arange(half, dtype=jnp.float32)
    freqs = jnp.exp(-jnp.log(jnp.float32(theta_base)) * 2.0 * index / HEAD_DIM)
    places = (starts[:, None] + jnp.arange(STEPS, dtype=jnp.int32)[None, :]).astype(jnp.float32)
    angle = places[:, :, None, None] * freqs[None, None, None, :]
    cosine = jnp.cos(angle)
    sine = jnp.sin(angle)
    first = normed[..., :half]
    second = normed[..., half:]
    return jnp.concatenate(
        [first * cosine - second * sine, second * cosine + first * sine], axis=-1
    )


def dot(left, right, dims):
    return lax.dot_general(left, right, (dims, ((), ())), preferred_element_type=f32)


def fold(rows):
    n = rows.shape[-2] // 2
    return jnp.concatenate([rows[..., :n, :], rows[..., n:, :]], axis=-1)


def unfold(rows):
    return jnp.concatenate([rows[..., :64], rows[..., 64:]], axis=-2)


def on_device(x, c, a, b, w, hidden, positions, gain):
    a_low = a.astype(bf16)
    b_low = b.astype(bf16)

    down_part = dot(x, a_low, ((1,), (0,))).astype(bf16)
    rows = jnp.concatenate([c, down_part], axis=1).reshape(8, 256, 128)
    send = jnp.concatenate([rows, jnp.broadcast_to(fold(b_low), (8, 32, 128))], axis=1)
    got = lax.all_to_all(send, TENSOR, 0, 0)
    c_rows = got[:, :256, :64]
    b_full = unfold(got[:, 256:])
    down = got[:, :256, 64:].astype(f32).sum(axis=0).astype(bf16)
    back = jnp.einsum("jtc,jkc->tk", c_rows, b_full, preferred_element_type=f32).astype(bf16)
    up_part = jnp.einsum("tk,jtc->jkc", down, c_rows, preferred_element_type=f32).astype(bf16)

    send = jnp.concatenate([jnp.broadcast_to(fold(back), (8, 128, 128)), fold(up_part)], axis=1)
    got = lax.all_to_all(send, TENSOR, 0, 0)
    back_all = unfold(got[:, :128]).reshape(2048, 64)
    up_part = got[:, 128:].astype(f32).sum(axis=0)
    down_part = dot(back_all, x, ((0,), (0,)))

    flat = hidden.reshape(4, 2, 128, 512)
    i0, i1, i2 = (lax.axis_index(n) for n in ("t0", "t1", "t2"))
    weight = jnp.concatenate([w, a_low, jnp.zeros_like(a_low)], axis=1)

    def project(which):
        part = lax.dynamic_index_in_dim(flat, which, 1, keepdims=False).reshape(512, 512)
        return dot(part, weight, ((1,), (0,))).astype(bf16)

    sent = project(1 - i0).reshape(2, 2, 128, 640)
    kept = project(i0).reshape(2, 2, 128, 640)

    tiles = down_part.reshape(8, 8, 4, 128).transpose(0, 2, 1, 3).reshape(32, 8, 128)
    send = jnp.concatenate(
        [tiles, up_part[:, None, :], jnp.zeros((32, 7, 128), f32)], axis=1
    ).astype(bf16)
    send, sent, kept = lax.optimization_barrier((send, sent, kept))
    came = lax.ppermute(sent, "t0", SWAP)
    got = lax.all_to_all(send, PLANE, 0, 0)
    mine = got.astype(f32).sum(axis=0).astype(bf16)
    mine, came = lax.optimization_barrier((mine, came))

    kept = kept + came
    sent = lax.dynamic_index_in_dim(kept, 1 - i1, 1, keepdims=False)
    kept = lax.dynamic_index_in_dim(kept, i1, 1, keepdims=False)
    mine, sent, kept = lax.optimization_barrier((mine, sent, kept))
    came = lax.ppermute(sent, "t1", SWAP)
    other = lax.ppermute(mine, "zh", SWAP)
    mine = (mine.astype(f32) + other.astype(f32)).astype(bf16)
    mine, came = lax.optimization_barrier((mine, came))

    kept = kept + came
    sent = lax.dynamic_index_in_dim(kept, 1 - i2, 0, keepdims=False)
    kept = lax.dynamic_index_in_dim(kept, i2, 0, keepdims=False)
    send = jnp.broadcast_to(mine, (32, 16, 128))
    send, sent, kept = lax.optimization_barrier((send, sent, kept))
    came = lax.ppermute(sent, "t2", SWAP)
    got = lax.all_to_all(send, PLANE, 0, 0)
    got, came = lax.optimization_barrier((got, came))
    kept = kept.astype(f32) + came.astype(f32)

    tiles = got[:, :8].reshape(8, 4, 8, 128).transpose(0, 2, 1, 3).reshape(64, 512)
    up_low = got[:, 8]
    down_grad = adapter_scale * tiles.T.astype(f32)
    up_grad = adapter_scale * unfold(up_low.astype(f32))
    square = jnp.sum(down_grad * down_grad) + jnp.sum(up_grad * up_grad)
    high = square.astype(bf16)
    low = (square - high.astype(f32)).astype(bf16)
    rank_part = dot(hidden.reshape(1024, 512), tiles, ((1,), (1,))).astype(bf16)
    scalars = jnp.concatenate([jnp.full((8, 8, 128), high), jnp.full((8, 8, 128), low)], axis=1)
    send = jnp.concatenate(
        [fold(rank_part.reshape(8, 128, 64)), jnp.broadcast_to(up_low, (8, 32, 128)), scalars],
        axis=1,
    )
    got = lax.all_to_all(send, TENSOR, 0, 0)
    total = jnp.sum(got[:, 96, 0].astype(f32) + got[:, 104, 0].astype(f32))
    factor = step_length / jnp.sqrt(total + epsilon)
    updated_down = a - factor * down_grad
    updated_up = b - factor * up_grad

    rank_new = unfold(got[:, :64].astype(f32).sum(axis=0)) * adapter_scale
    base = kept[:, :512]
    rank_act = kept[:, 512:576] - factor * rank_new
    return base, rank_act, b_full, got[:, 64:96], factor, updated_down, updated_up, positions, gain


def finish(base, rank_act, b_full, up_all, factor, updated_down, updated_up, positions, gain):
    up_new = (b_full.astype(f32) - factor * adapter_scale * unfold(up_all).astype(f32)).astype(bf16)
    up_new = up_new.transpose(1, 0, 2).reshape(64, 512)
    proj = base + adapter_scale * jnp.dot(
        rank_act, up_new.astype(f32), precision=lax.Precision.HIGHEST, preferred_element_type=f32
    )
    own = positions.shape[0]
    heads = proj.reshape(own, STEPS, KV_HEADS, HEAD_DIM)
    normed = heads * lax.rsqrt(jnp.mean(heads * heads, axis=-1, keepdims=True) + epsilon) * gain
    keys = rotate(normed, positions).reshape(own, STEPS, KV_HEADS * HEAD_DIM).astype(bf16)
    return keys, updated_down, updated_up


def whole(*args):
    return finish(*on_device(*args))


def solution(mesh):
    names = ("y", "x", "zh", "core") + TENSOR
    fine = Mesh(mesh.devices.reshape(4, 4, 2, 2, 2, 2, 2), names)
    dp = ("y", "x", "zh", "core")
    in_specs = (
        P(dp, TENSOR),
        P(dp, TENSOR),
        P(TENSOR, None),
        P(None, TENSOR),
        P(TENSOR, None),
        P(dp, None, TENSOR),
        P(dp + TENSOR),
        P(),
    )
    out_specs = (P(dp + TENSOR, None, None), P(TENSOR, None), P(None, TENSOR))
    return jax.shard_map(whole, mesh=fine, in_specs=in_specs, out_specs=out_specs, check_vma=False)
```

```python
import jax
import jax.numpy as jnp
from jax import lax
from jax.experimental import pallas as pl
from jax.experimental.pallas import tpu as pltpu
from jax.sharding import Mesh
from jax.sharding import PartitionSpec as P

HEAD_DIM = 128
KV_HEADS = 4
STEPS = 4
RANK = 64

adapter_scale = 2.0
step_length = 8.0
epsilon = 1e-06
theta_base = 1000000.0

TENSOR = ("t2", "t1", "t0")
QUAD = ("t1", "t0")
PLANE = ("y", "x", "core")
DP = ("y", "x", "zh", "core")
SWAP = [(0, 1), (1, 0)]
VMEM = pl.BlockSpec(memory_space=pltpu.VMEM)
SMALL = pltpu.CompilerParams(vmem_limit_bytes=16 * 1024 * 1024)
bf16 = jnp.bfloat16
f32 = jnp.float32


def dot(left, right, contract, precision=None):
    return lax.dot_general(
        left, right, ((contract[:1], contract[1:]), ((), ())),
        precision=precision, preferred_element_type=f32,
    )


def struct(shape, dtype):
    return jax.ShapeDtypeStruct(shape, dtype)


def partials_kernel(
    x_ref, ct_ref, at_ref, b_ref, out_ref, x_in, ct_in, at_in, b_in, sent, x_sems, sems, out_sems
):
    small = [
        pltpu.make_async_copy(source, target, sems.at[i])
        for i, (source, target) in enumerate(((at_ref, at_in), (b_ref, b_in), (ct_ref, ct_in)))
    ]
    large = [
        pltpu.make_async_copy(
            x_ref.at[pl.ds(512 * q, 512)], x_in.at[pl.ds(512 * q, 512)], x_sems.at[q]
        )
        for q in range(4)
    ]
    back = [pltpu.make_async_copy(sent.at[q], out_ref.at[q], out_sems.at[q]) for q in range(4)]
    for copy in small + large:
        copy.start()
    for copy in small:
        copy.wait()
    a = at_in[...].T.astype(bf16)
    b = b_in[...].astype(bf16)
    for q in range(4):
        sent[q, RANK:] = dot(b, ct_in[:, 512 * q : 512 * (q + 1)], (1, 0)).astype(bf16)
    for q in range(4):
        large[q].wait()
        sent[q, :RANK] = dot(x_in[512 * q : 512 * (q + 1)], a, (1, 0)).T.astype(bf16)
        back[q].start()
    for copy in back:
        copy.wait()


def partials(x, ct, at, b):
    return pl.pallas_call(
        partials_kernel,
        in_specs=[pl.BlockSpec(memory_space=pl.ANY)] * 4,
        out_specs=pl.BlockSpec(memory_space=pl.ANY),
        out_shape=struct((4, 2 * RANK, 512), bf16),
        scratch_shapes=[
            pltpu.VMEM((2048, 512), bf16),
            pltpu.VMEM((RANK, 2048), bf16),
            pltpu.VMEM((RANK, 512), f32),
            pltpu.VMEM((RANK, RANK), f32),
            pltpu.VMEM((4, 2 * RANK, 512), bf16),
            pltpu.SemaphoreType.DMA((4,)),
            pltpu.SemaphoreType.DMA((3,)),
            pltpu.SemaphoreType.DMA((4,)),
        ],
        name="partials",
    )(x, ct, at, b)


def base_kernel(me_ref, h_ref, w_ref, at_ref, send_ref, keep_ref):
    rows = h_ref[...]
    base = dot(rows, w_ref[...], (1, 0)).astype(bf16)
    acts = dot(rows, at_ref[...].T.astype(bf16), (1, 0)).T.astype(bf16)

    def write(out_ref):
        for k in range(KV_HEADS):
            out_ref[0, 128 * k : 128 * (k + 1)] = base[:, 128 * k : 128 * (k + 1)]
        out_ref[0, 512:] = acts

    @pl.when(pl.program_id(0) == 0)
    def _():
        write(send_ref)

    @pl.when(pl.program_id(0) == 1)
    def _():
        write(keep_ref)


def base_parts(me, flat, w, at):
    def rows(s, m, me_ref):
        t0 = jnp.where(s == 0, 1 - me_ref[0], me_ref[0])
        return (m % 2) * 4 + (m // 2) * 2 + t0, 0

    return pl.pallas_call(
        base_kernel,
        grid_spec=pltpu.PrefetchScalarGridSpec(
            num_scalar_prefetch=1,
            grid=(2, 4),
            in_specs=[
                pl.BlockSpec((128, 512), rows),
                pl.BlockSpec((512, 512), lambda s, m, me_ref: (0, 0)),
                pl.BlockSpec((RANK, 512), lambda s, m, me_ref: (0, 0)),
            ],
            out_specs=[
                pl.BlockSpec((1, 576, 128), lambda s, m, me_ref: (jnp.where(s == 0, m, 3), 0, 0)),
                pl.BlockSpec((1, 576, 128), lambda s, m, me_ref: (jnp.where(s == 0, 0, m), 0, 0)),
            ],
        ),
        out_shape=(struct((4, 576, 128), bf16), struct((4, 576, 128), bf16)),
        cost_estimate=pl.CostEstimate(flops=2 * 1024 * 512 * 576, bytes_accessed=3000000, transcendentals=0),
        compiler_params=SMALL,
        name="base",
    )(me, flat, w, at)


def grads_kernel(acts_ref, x_ref, ct_ref, out_ref):
    up = jnp.zeros((RANK, RANK), f32)
    for q in range(4):
        up += dot(acts_ref[q, :RANK], ct_ref[:, 512 * q : 512 * (q + 1)], (1, 1))
    folded = jnp.concatenate([up[:32], up[32:]], axis=1)
    down = jnp.zeros((RANK, 512), f32)
    for q in range(4):
        down += dot(acts_ref[q, RANK:], x_ref[512 * q : 512 * (q + 1)], (1, 0))
    for c in range(32):
        r, k = c // 4, c % 4
        tile = down[8 * r : 8 * r + 8, 128 * k : 128 * (k + 1)]
        row = jnp.broadcast_to(folded[c : c + 1], (8, 128))
        both = jnp.concatenate([tile, row], axis=0).astype(bf16)
        out_ref[c] = both


def gradients(acts, x, ct):
    return pl.pallas_call(
        grads_kernel,
        in_specs=[VMEM] * 3,
        out_specs=VMEM,
        out_shape=struct((32, 16, 128), bf16),
        compiler_params=SMALL,
        name="gradients",
    )(acts, x, ct)


def rank_kernel(got_ref, h_ref, b_ref, send_ref, down_ref, up_ref):
    for c in range(32):
        r, k = c // 4, c % 4
        both = got_ref[c].astype(f32)
        down_ref[8 * r : 8 * r + 8, 128 * k : 128 * (k + 1)] = both[:8]
        up_ref[c : c + 1] = both[8:9]
    down = down_ref[...]
    up = up_ref[...]
    square = jnp.sum(down * down) + jnp.sum(up * up)
    square = jnp.full((16, 128), square, f32)
    high = square.astype(bf16).astype(f32)
    first = lax.broadcasted_iota(jnp.int32, (16, 128), 0) < 8
    scalars = jnp.where(first, high, square - high).astype(bf16)
    low_b = b_ref[...].astype(bf16).astype(f32)
    small = jnp.concatenate(
        [up.astype(bf16), jnp.concatenate([low_b[:32], low_b[32:]], axis=1).astype(bf16), scalars],
        axis=0,
    )
    down = down.T.astype(bf16)
    for j in range(8):
        acts = dot(h_ref[128 * j : 128 * (j + 1)], down, (1, 0))
        send_ref[j, :RANK] = acts.T.astype(bf16)
        send_ref[j, RANK:] = small


def rank_parts(got, flat, b):
    return pl.pallas_call(
        rank_kernel,
        in_specs=[VMEM] * 3,
        out_specs=[VMEM] * 3,
        out_shape=(struct((8, 144, 128), bf16), struct((RANK, 512), f32), struct((32, 128), f32)),
        compiler_params=SMALL,
        name="rank",
    )(got, flat, b)


def finish_kernel(
    got_ref, kept_ref, came_ref, down_ref, up_ref, at_ref, b_ref, cos_ref, sin_ref, gain_ref,
    keys_ref, down_out_ref, up_out_ref,
):
    total = jnp.zeros((8, 128), f32)
    acts = jnp.zeros((RANK, 128), f32)
    for j in range(8):
        part = got_ref[j, 128:].astype(f32)
        total += part[:8] + part[8:]
        acts += got_ref[j, :RANK].astype(f32)
    total = total[:1] * (adapter_scale * adapter_scale)
    move = adapter_scale * (step_length / jnp.sqrt(total + epsilon))
    down_out_ref[...] = at_ref[...] - move[:, :1] * down_ref[...]
    up = up_ref[...]
    up_out_ref[...] = b_ref[...] - move[:, :RANK] * jnp.concatenate([up[:, :RANK], up[:, RANK:]], axis=0)
    base = kept_ref[...].astype(f32) + came_ref[...].astype(f32)
    rank_act = base[512:] - move * acts
    for k in range(KV_HEADS):
        pair = []
        for j in (2 * k, 2 * k + 1):
            low = got_ref[j, 96:128].astype(f32) - move * got_ref[j, 64:96].astype(f32)
            pair.append(jnp.concatenate([low[:, :RANK], low[:, RANK:]], axis=0))
        up_new = jnp.concatenate(pair, axis=1).astype(bf16).astype(f32)
        head = base[128 * k : 128 * (k + 1)] + adapter_scale * dot(
            rank_act, up_new, (0, 0), lax.Precision.HIGHEST
        )
        mean = jnp.mean(head * head, axis=-1, keepdims=True)
        head = head * lax.rsqrt(mean + epsilon) * gain_ref[...]
        turned = head * cos_ref[...] + pltpu.roll(head, 64, 1) * sin_ref[...]
        keys_ref[:, :, 128 * k : 128 * (k + 1)] = turned.reshape(32, STEPS, 128).astype(bf16)


def finish(got, kept, came, down, up, at, b, cosine, sine, gain):
    return pl.pallas_call(
        finish_kernel,
        in_specs=[VMEM] * 10,
        out_specs=[VMEM] * 3,
        out_shape=(struct((32, STEPS, 512), bf16), struct((RANK, 512), f32), struct((RANK, RANK), f32)),
        compiler_params=SMALL,
        name="finish",
    )(got, kept, came, down, up, at, b, cosine, sine, gain)


def tables(positions):
    half = HEAD_DIM // 2
    index = jnp.arange(half, dtype=f32)
    freqs = jnp.exp(-jnp.log(f32(theta_base)) * 2.0 * index / HEAD_DIM)
    places = (positions[:, None] + jnp.arange(STEPS, dtype=jnp.int32)[None, :]).astype(f32)
    angle = places.reshape(-1, 1) * freqs[None, :]
    cosine = jnp.cos(angle)
    sine = jnp.sin(angle)
    return jnp.concatenate([cosine, cosine], axis=1), jnp.concatenate([-sine, sine], axis=1)


def on_device(x, c, a, b, w, hidden, positions, gain):
    at = a.T
    ct = c.T
    flat = hidden.reshape(1024, 512)

    i0, i1, i2 = (lax.axis_index(n) for n in ("t0", "t1", "t2"))

    got = lax.all_to_all(partials(x, ct, at, b), QUAD, 0, 0)
    mine = got.astype(f32).sum(axis=0).astype(bf16)
    mine, flat = lax.optimization_barrier((mine, flat))
    other = lax.ppermute(mine, "t2", SWAP)
    sent, kept = base_parts(i0.reshape(1), flat, w, at)
    other, sent, kept = lax.optimization_barrier((other, sent, kept))
    mine = (mine.astype(f32) + other.astype(f32)).astype(bf16)
    acts = lax.all_to_all(jnp.broadcast_to(mine, (4, 128, 512)), QUAD, 0, 0)

    grads = gradients(acts, x, ct)
    grads, sent, kept = lax.optimization_barrier((grads, sent, kept))
    came = lax.ppermute(sent, "t0", SWAP)
    got = lax.all_to_all(grads, PLANE, 0, 0)
    mine = got.astype(f32).sum(axis=0).astype(bf16)
    mine, came = lax.optimization_barrier((mine, came))

    def part(i):
        pick = lambda v: lax.dynamic_index_in_dim(v.reshape(2, 2, 576, 128), i, 0, keepdims=False)
        return pick(kept) + pick(came)

    mine, sent1, kept1 = lax.optimization_barrier((mine, part(1 - i1), part(i1)))
    came1 = lax.ppermute(sent1, "t1", SWAP)
    other = lax.ppermute(mine, "zh", SWAP)
    mine = (mine.astype(f32) + other.astype(f32)).astype(bf16)
    mine, came1 = lax.optimization_barrier((mine, came1))

    def half(i):
        pick = lambda v: lax.dynamic_index_in_dim(v, i, 0, keepdims=False)
        return pick(kept1) + pick(came1)

    send, sent2, kept2 = lax.optimization_barrier(
        (jnp.broadcast_to(mine, (32, 16, 128)), half(1 - i2), half(i2))
    )
    came2 = lax.ppermute(sent2, "t2", SWAP)
    got = lax.all_to_all(send, PLANE, 0, 0)

    send, down, up = rank_parts(got, flat, b)
    send, came2 = lax.optimization_barrier((send, came2))
    got = lax.all_to_all(send, TENSOR, 0, 0)
    cosine, sine = tables(positions)
    keys, new_down, new_up = finish(got, kept2, came2, down, up, at, b, cosine, sine, gain.reshape(1, 128))
    return keys, new_down.T, new_up


def solution(mesh):
    names = ("y", "x", "zh", "core") + TENSOR
    fine = Mesh(mesh.devices.reshape(4, 4, 2, 2, 2, 2, 2), names)
    in_specs = (
        P(DP, TENSOR),
        P(DP, TENSOR),
        P(TENSOR, None),
        P(None, TENSOR),
        P(TENSOR, None),
        P(DP, None, TENSOR),
        P(DP + TENSOR),
        P(),
    )
    out_specs = (P(DP + TENSOR, None, None), P(TENSOR, None), P(None, TENSOR))
    return jax.shard_map(on_device, mesh=fine, in_specs=in_specs, out_specs=out_specs, check_vma=False)
```

```python
import jax
import jax.numpy as jnp
from jax import lax
from jax.experimental import pallas as pl
from jax.experimental.pallas import tpu as pltpu
from jax.sharding import Mesh
from jax.sharding import PartitionSpec as P

HEAD_DIM = 128
KV_HEADS = 4
STEPS = 4
RANK = 64

adapter_scale = 2.0
step_length = 8.0
epsilon = 1e-06
theta_base = 1000000.0

TENSOR = ("t2", "t1", "t0")
QUAD = ("t1", "t0")
PLANE = ("y", "x", "core")
DP = ("y", "x", "zh", "core")
SWAP = [(0, 1), (1, 0)]
VMEM = pl.BlockSpec(memory_space=pltpu.VMEM)
SMALL = pltpu.CompilerParams(vmem_limit_bytes=16 * 1024 * 1024)
bf16 = jnp.bfloat16
f32 = jnp.float32


def dot(left, right, contract, precision=None):
    return lax.dot_general(
        left, right, ((contract[:1], contract[1:]), ((), ())),
        precision=precision, preferred_element_type=f32,
    )


def struct(shape, dtype):
    return jax.ShapeDtypeStruct(shape, dtype)


def partials_kernel(
    x_ref, ct_ref, at_ref, b_ref, out_ref, x_in, ct_in, at_in, b_in, sent, x_sems, sems, out_sems
):
    small = [
        pltpu.make_async_copy(source, target, sems.at[i])
        for i, (source, target) in enumerate(((at_ref, at_in), (b_ref, b_in), (ct_ref, ct_in)))
    ]
    large = [
        pltpu.make_async_copy(
            x_ref.at[pl.ds(512 * q, 512)], x_in.at[pl.ds(512 * q, 512)], x_sems.at[q]
        )
        for q in range(4)
    ]
    back = [pltpu.make_async_copy(sent.at[q], out_ref.at[q], out_sems.at[q]) for q in range(4)]
    for copy in small + large:
        copy.start()
    for copy in small:
        copy.wait()
    a = at_in[...].T.astype(bf16)
    b = b_in[...].astype(bf16)
    for q in range(4):
        sent[q, RANK:] = dot(b, ct_in[:, 512 * q : 512 * (q + 1)], (1, 0)).astype(bf16)
    for q in range(4):
        large[q].wait()
        sent[q, :RANK] = dot(x_in[512 * q : 512 * (q + 1)], a, (1, 0)).T.astype(bf16)
        back[q].start()
    for copy in back:
        copy.wait()


def partials(x, ct, at, b):
    return pl.pallas_call(
        partials_kernel,
        in_specs=[pl.BlockSpec(memory_space=pl.ANY)] * 4,
        out_specs=pl.BlockSpec(memory_space=pl.ANY),
        out_shape=struct((4, 2 * RANK, 512), bf16),
        scratch_shapes=[
            pltpu.VMEM((2048, 512), bf16),
            pltpu.VMEM((RANK, 2048), bf16),
            pltpu.VMEM((RANK, 512), f32),
            pltpu.VMEM((RANK, RANK), f32),
            pltpu.VMEM((4, 2 * RANK, 512), bf16),
            pltpu.SemaphoreType.DMA((4,)),
            pltpu.SemaphoreType.DMA((3,)),
            pltpu.SemaphoreType.DMA((4,)),
        ],
        name="partials",
    )(x, ct, at, b)


def base_kernel(me_ref, h_ref, w_ref, at_ref, send_ref, keep_ref):
    rows = h_ref[...]
    base = dot(rows, w_ref[...], (1, 0)).astype(bf16)
    acts = dot(rows, at_ref[...].T.astype(bf16), (1, 0)).T.astype(bf16)

    def write(out_ref):
        for k in range(KV_HEADS):
            out_ref[0, 128 * k : 128 * (k + 1)] = base[:, 128 * k : 128 * (k + 1)]
        out_ref[0, 512:] = acts

    @pl.when(pl.program_id(0) == 0)
    def _():
        write(send_ref)

    @pl.when(pl.program_id(0) == 1)
    def _():
        write(keep_ref)


def base_parts(me, flat, w, at):
    def rows(s, m, me_ref):
        t0 = jnp.where(s == 0, 1 - me_ref[0], me_ref[0])
        return (m % 2) * 4 + (m // 2) * 2 + t0, 0

    return pl.pallas_call(
        base_kernel,
        grid_spec=pltpu.PrefetchScalarGridSpec(
            num_scalar_prefetch=1,
            grid=(2, 4),
            in_specs=[
                pl.BlockSpec((128, 512), rows),
                pl.BlockSpec((512, 512), lambda s, m, me_ref: (0, 0)),
                pl.BlockSpec((RANK, 512), lambda s, m, me_ref: (0, 0)),
            ],
            out_specs=[
                pl.BlockSpec((1, 576, 128), lambda s, m, me_ref: (jnp.where(s == 0, m, 3), 0, 0)),
                pl.BlockSpec((1, 576, 128), lambda s, m, me_ref: (jnp.where(s == 0, 0, m), 0, 0)),
            ],
        ),
        out_shape=(struct((4, 576, 128), bf16), struct((4, 576, 128), bf16)),
        cost_estimate=pl.CostEstimate(flops=2 * 1024 * 512 * 576, bytes_accessed=3000000, transcendentals=0),
        compiler_params=SMALL,
        name="base",
    )(me, flat, w, at)


def grads_kernel(acts_ref, x_ref, ct_ref, out_ref):
    up = jnp.zeros((RANK, RANK), f32)
    for q in range(4):
        up += dot(acts_ref[q, :RANK], ct_ref[:, 512 * q : 512 * (q + 1)], (1, 1))
    folded = jnp.concatenate([up[:32], up[32:]], axis=1)
    down = jnp.zeros((RANK, 512), f32)
    for q in range(4):
        down += dot(acts_ref[q, RANK:], x_ref[512 * q : 512 * (q + 1)], (1, 0))
    for c in range(32):
        r, k = c // 4, c % 4
        tile = down[8 * r : 8 * r + 8, 128 * k : 128 * (k + 1)]
        row = jnp.broadcast_to(folded[c : c + 1], (8, 128))
        both = jnp.concatenate([tile, row], axis=0).astype(bf16)
        out_ref[c] = both


def gradients(acts, x, ct):
    return pl.pallas_call(
        grads_kernel,
        in_specs=[VMEM] * 3,
        out_specs=VMEM,
        out_shape=struct((32, 16, 128), bf16),
        compiler_params=SMALL,
        name="gradients",
    )(acts, x, ct)


def rank_kernel(got_ref, h_ref, b_ref, send_ref, down_ref, up_ref):
    for c in range(32):
        r, k = c // 4, c % 4
        both = got_ref[c].astype(f32)
        down_ref[8 * r : 8 * r + 8, 128 * k : 128 * (k + 1)] = both[:8]
        up_ref[c : c + 1] = both[8:9]
    down = down_ref[...]
    up = up_ref[...]
    square = jnp.sum(down * down) + jnp.sum(up * up)
    square = jnp.full((16, 128), square, f32)
    high = square.astype(bf16).astype(f32)
    first = lax.broadcasted_iota(jnp.int32, (16, 128), 0) < 8
    scalars = jnp.where(first, high, square - high).astype(bf16)
    low_b = b_ref[...].astype(bf16).astype(f32)
    small = jnp.concatenate(
        [up.astype(bf16), jnp.concatenate([low_b[:32], low_b[32:]], axis=1).astype(bf16), scalars],
        axis=0,
    )
    down = down.T.astype(bf16)
    for j in range(8):
        acts = dot(h_ref[128 * j : 128 * (j + 1)], down, (1, 0))
        send_ref[j, :RANK] = acts.T.astype(bf16)
        send_ref[j, RANK:] = small


def rank_parts(got, flat, b):
    return pl.pallas_call(
        rank_kernel,
        in_specs=[VMEM] * 3,
        out_specs=[VMEM] * 3,
        out_shape=(struct((8, 144, 128), bf16), struct((RANK, 512), f32), struct((32, 128), f32)),
        compiler_params=SMALL,
        name="rank",
    )(got, flat, b)


def finish_kernel(
    got_ref, kept_ref, came_ref, down_ref, up_ref, at_ref, b_ref, cos_ref, sin_ref, gain_ref,
    keys_ref, down_out_ref, up_out_ref,
):
    total = jnp.zeros((8, 128), f32)
    acts = jnp.zeros((RANK, 128), f32)
    for j in range(8):
        part = got_ref[j, 128:].astype(f32)
        total += part[:8] + part[8:]
        acts += got_ref[j, :RANK].astype(f32)
    total = total[:1] * (adapter_scale * adapter_scale)
    move = adapter_scale * (step_length / jnp.sqrt(total + epsilon))
    down_out_ref[...] = at_ref[...] - move[:, :1] * down_ref[...]
    up = up_ref[...]
    up_out_ref[...] = b_ref[...] - move[:, :RANK] * jnp.concatenate([up[:, :RANK], up[:, RANK:]], axis=0)
    base = kept_ref[...].astype(f32) + came_ref[...].astype(f32)
    rank_act = base[512:] - move * acts
    for k in range(KV_HEADS):
        pair = []
        for j in (2 * k, 2 * k + 1):
            low = got_ref[j, 96:128].astype(f32) - move * got_ref[j, 64:96].astype(f32)
            pair.append(jnp.concatenate([low[:, :RANK], low[:, RANK:]], axis=0))
        up_new = jnp.concatenate(pair, axis=1).astype(bf16).astype(f32)
        head = base[128 * k : 128 * (k + 1)] + adapter_scale * dot(
            rank_act, up_new, (0, 0), lax.Precision.HIGHEST
        )
        mean = jnp.mean(head * head, axis=-1, keepdims=True)
        head = head * lax.rsqrt(mean + epsilon) * gain_ref[...]
        turned = head * cos_ref[...] + pltpu.roll(head, 64, 1) * sin_ref[...]
        keys_ref[:, :, 128 * k : 128 * (k + 1)] = turned.reshape(32, STEPS, 128).astype(bf16)


def finish(got, kept, came, down, up, at, b, cosine, sine, gain):
    return pl.pallas_call(
        finish_kernel,
        in_specs=[VMEM] * 10,
        out_specs=[VMEM] * 3,
        out_shape=(struct((32, STEPS, 512), bf16), struct((RANK, 512), f32), struct((RANK, RANK), f32)),
        compiler_params=SMALL,
        name="finish",
    )(got, kept, came, down, up, at, b, cosine, sine, gain)


def tables(positions):
    half = HEAD_DIM // 2
    index = jnp.arange(half, dtype=f32)
    freqs = jnp.exp(-jnp.log(f32(theta_base)) * 2.0 * index / HEAD_DIM)
    places = (positions[:, None] + jnp.arange(STEPS, dtype=jnp.int32)[None, :]).astype(f32)
    angle = places.reshape(-1, 1) * freqs[None, :]
    cosine = jnp.cos(angle)
    sine = jnp.sin(angle)
    return jnp.concatenate([cosine, cosine], axis=1), jnp.concatenate([-sine, sine], axis=1)


def on_device(x, c, a, b, w, hidden, positions, gain):
    at = a.T
    ct = c.T
    flat = hidden.reshape(1024, 512)

    i0, i1, i2 = (lax.axis_index(n) for n in ("t0", "t1", "t2"))

    got = lax.all_to_all(partials(x, ct, at, b), QUAD, 0, 0)
    mine = got.astype(f32).sum(axis=0).astype(bf16)
    mine, flat = lax.optimization_barrier((mine, flat))
    other = lax.ppermute(mine, "t2", SWAP)
    sent, kept = base_parts(i0.reshape(1), flat, w, at)
    other, sent, kept = lax.optimization_barrier((other, sent, kept))
    mine = (mine.astype(f32) + other.astype(f32)).astype(bf16)
    acts = lax.all_to_all(jnp.broadcast_to(mine, (4, 128, 512)), QUAD, 0, 0)

    grads = gradients(acts, x, ct)
    grads, sent, kept = lax.optimization_barrier((grads, sent, kept))
    came = lax.ppermute(sent, "t0", SWAP)
    got = lax.all_to_all(grads, PLANE, 0, 0)

    def part(i):
        pick = lambda v: lax.dynamic_index_in_dim(v.reshape(2, 2, 576, 128), i, 0, keepdims=False)
        return pick(kept) + pick(came)

    sent1, kept1 = part(1 - i1), part(i1)
    came1 = lax.ppermute(sent1, "t1", SWAP)
    got, _ = lax.optimization_barrier((got, sent1))
    mine = got.astype(f32).sum(axis=0).astype(bf16)
    other = lax.ppermute(mine, "zh", SWAP)
    mine = (mine.astype(f32) + other.astype(f32)).astype(bf16)
    mine, came1 = lax.optimization_barrier((mine, came1))

    def half(i):
        pick = lambda v: lax.dynamic_index_in_dim(v, i, 0, keepdims=False)
        return pick(kept1) + pick(came1)

    send, sent2, kept2 = lax.optimization_barrier(
        (jnp.broadcast_to(mine, (32, 16, 128)), half(1 - i2), half(i2))
    )
    came2 = lax.ppermute(sent2, "t2", SWAP)
    got = lax.all_to_all(send, PLANE, 0, 0)

    send, down, up = rank_parts(got, flat, b)
    send, came2 = lax.optimization_barrier((send, came2))
    got = lax.all_to_all(send, TENSOR, 0, 0)
    cosine, sine = tables(positions)
    keys, new_down, new_up = finish(got, kept2, came2, down, up, at, b, cosine, sine, gain.reshape(1, 128))
    return keys, new_down.T, new_up


def solution(mesh):
    names = ("y", "x", "zh", "core") + TENSOR
    fine = Mesh(mesh.devices.reshape(4, 4, 2, 2, 2, 2, 2), names)
    in_specs = (
        P(DP, TENSOR),
        P(DP, TENSOR),
        P(TENSOR, None),
        P(None, TENSOR),
        P(TENSOR, None),
        P(DP, None, TENSOR),
        P(DP + TENSOR),
        P(),
    )
    out_specs = (P(DP + TENSOR, None, None), P(TENSOR, None), P(None, TENSOR))
    return jax.shard_map(on_device, mesh=fine, in_specs=in_specs, out_specs=out_specs, check_vma=False)
```

```python
import jax
import jax.numpy as jnp
from jax import lax
from jax.experimental import pallas as pl
from jax.experimental.pallas import tpu as pltpu
from jax.sharding import Mesh
from jax.sharding import PartitionSpec as P

HEAD_DIM = 128
KV_HEADS = 4
STEPS = 4
RANK = 64

adapter_scale = 2.0
step_length = 8.0
epsilon = 1e-06
theta_base = 1000000.0

TENSOR = ("t2", "t1", "t0")
QUAD = ("t1", "t0")
PLANE = ("y", "x", "core")
DP = ("y", "x", "zh", "core")
SWAP = [(0, 1), (1, 0)]
VMEM = pl.BlockSpec(memory_space=pltpu.VMEM)
SMALL = pltpu.CompilerParams(vmem_limit_bytes=6 * 1024 * 1024)
bf16 = jnp.bfloat16
f32 = jnp.float32


def dot(left, right, contract, precision=None):
    return lax.dot_general(
        left, right, ((contract[:1], contract[1:]), ((), ())),
        precision=precision, preferred_element_type=f32,
    )


def struct(shape, dtype):
    return jax.ShapeDtypeStruct(shape, dtype)


def partials_kernel(
    x_ref, ct_ref, at_ref, b_ref, out_ref, x_in, ct_in, at_in, b_in, sent, x_sems, sems, out_sems
):
    small = [
        pltpu.make_async_copy(source, target, sems.at[i])
        for i, (source, target) in enumerate(((at_ref, at_in), (b_ref, b_in), (ct_ref, ct_in)))
    ]
    large = [
        pltpu.make_async_copy(
            x_ref.at[pl.ds(512 * q, 512)], x_in.at[pl.ds(512 * q, 512)], x_sems.at[q]
        )
        for q in range(4)
    ]
    back = [pltpu.make_async_copy(sent.at[q], out_ref.at[q], out_sems.at[q]) for q in range(4)]
    for copy in small + large:
        copy.start()
    for copy in small:
        copy.wait()
    a = at_in[...].T.astype(bf16)
    b = b_in[...].astype(bf16)
    for q in range(4):
        sent[q, RANK:] = dot(b, ct_in[:, 512 * q : 512 * (q + 1)], (1, 0)).astype(bf16)
    for q in range(4):
        large[q].wait()
        sent[q, :RANK] = dot(x_in[512 * q : 512 * (q + 1)], a, (1, 0)).T.astype(bf16)
        back[q].start()
    for copy in back:
        copy.wait()


def partials(x, ct, at, b):
    return pl.pallas_call(
        partials_kernel,
        in_specs=[pl.BlockSpec(memory_space=pl.ANY)] * 4,
        out_specs=pl.BlockSpec(memory_space=pl.ANY),
        out_shape=struct((4, 2 * RANK, 512), bf16),
        scratch_shapes=[
            pltpu.VMEM((2048, 512), bf16),
            pltpu.VMEM((RANK, 2048), bf16),
            pltpu.VMEM((RANK, 512), f32),
            pltpu.VMEM((RANK, RANK), f32),
            pltpu.VMEM((4, 2 * RANK, 512), bf16),
            pltpu.SemaphoreType.DMA((4,)),
            pltpu.SemaphoreType.DMA((3,)),
            pltpu.SemaphoreType.DMA((4,)),
        ],
        name="partials",
    )(x, ct, at, b)


def base_kernel(me_ref, h_ref, w_ref, at_ref, send_ref, keep_ref):
    rows = h_ref[...]
    base = dot(rows, w_ref[...], (1, 0)).astype(bf16)
    acts = dot(rows, at_ref[...].T.astype(bf16), (1, 0)).T.astype(bf16)

    def write(out_ref):
        for k in range(KV_HEADS):
            out_ref[0, 128 * k : 128 * (k + 1)] = base[:, 128 * k : 128 * (k + 1)]
        out_ref[0, 512:] = acts

    @pl.when(pl.program_id(0) == 0)
    def _():
        write(send_ref)

    @pl.when(pl.program_id(0) == 1)
    def _():
        write(keep_ref)


def base_parts(me, flat, w, at):
    def rows(s, m, me_ref):
        t0 = jnp.where(s == 0, 1 - me_ref[0], me_ref[0])
        return (m % 2) * 4 + (m // 2) * 2 + t0, 0

    return pl.pallas_call(
        base_kernel,
        grid_spec=pltpu.PrefetchScalarGridSpec(
            num_scalar_prefetch=1,
            grid=(2, 4),
            in_specs=[
                pl.BlockSpec((128, 512), rows),
                pl.BlockSpec((512, 512), lambda s, m, me_ref: (0, 0)),
                pl.BlockSpec((RANK, 512), lambda s, m, me_ref: (0, 0)),
            ],
            out_specs=[
                pl.BlockSpec((1, 576, 128), lambda s, m, me_ref: (jnp.where(s == 0, m, 3), 0, 0)),
                pl.BlockSpec((1, 576, 128), lambda s, m, me_ref: (jnp.where(s == 0, 0, m), 0, 0)),
            ],
        ),
        out_shape=(struct((4, 576, 128), bf16), struct((4, 576, 128), bf16)),
        cost_estimate=pl.CostEstimate(flops=2 * 1024 * 512 * 576, bytes_accessed=3000000, transcendentals=0),
        compiler_params=SMALL,
        name="base",
    )(me, flat, w, at)


def grads_kernel(acts_ref, x_ref, ct_ref, out_ref):
    up = jnp.zeros((RANK, RANK), f32)
    for q in range(4):
        up += dot(acts_ref[q, :RANK], ct_ref[:, 512 * q : 512 * (q + 1)], (1, 1))
    folded = jnp.concatenate([up[:32], up[32:]], axis=1)
    down = jnp.zeros((RANK, 512), f32)
    for q in range(4):
        down += dot(acts_ref[q, RANK:], x_ref[512 * q : 512 * (q + 1)], (1, 0))
    for c in range(32):
        r, k = c // 4, c % 4
        tile = down[8 * r : 8 * r + 8, 128 * k : 128 * (k + 1)]
        row = jnp.broadcast_to(folded[c : c + 1], (8, 128))
        both = jnp.concatenate([tile, row], axis=0).astype(bf16)
        out_ref[c] = both


def gradients(acts, x, ct):
    return pl.pallas_call(
        grads_kernel,
        in_specs=[VMEM] * 3,
        out_specs=VMEM,
        out_shape=struct((32, 16, 128), bf16),
        compiler_params=SMALL,
        name="gradients",
    )(acts, x, ct)


def rank_kernel(got_ref, h_ref, b_ref, send_ref, down_ref, up_ref):
    for c in range(32):
        r, k = c // 4, c % 4
        both = got_ref[c].astype(f32)
        down_ref[8 * r : 8 * r + 8, 128 * k : 128 * (k + 1)] = both[:8]
        up_ref[c : c + 1] = both[8:9]
    down = down_ref[...]
    up = up_ref[...]
    square = jnp.sum(down * down) + jnp.sum(up * up)
    square = jnp.full((16, 128), square, f32)
    high = square.astype(bf16).astype(f32)
    first = lax.broadcasted_iota(jnp.int32, (16, 128), 0) < 8
    scalars = jnp.where(first, high, square - high).astype(bf16)
    low_b = b_ref[...].astype(bf16).astype(f32)
    small = jnp.concatenate(
        [up.astype(bf16), jnp.concatenate([low_b[:32], low_b[32:]], axis=1).astype(bf16), scalars],
        axis=0,
    )
    down = down.T.astype(bf16)
    for j in range(8):
        acts = dot(h_ref[128 * j : 128 * (j + 1)], down, (1, 0))
        send_ref[j, :RANK] = acts.T.astype(bf16)
        send_ref[j, RANK:] = small


def rank_parts(got, flat, b):
    return pl.pallas_call(
        rank_kernel,
        in_specs=[VMEM] * 3,
        out_specs=[VMEM] * 3,
        out_shape=(struct((8, 144, 128), bf16), struct((RANK, 512), f32), struct((32, 128), f32)),
        compiler_params=SMALL,
        name="rank",
    )(got, flat, b)


def finish_kernel(
    got_ref, kept_ref, came_ref, down_ref, up_ref, at_ref, b_ref, cos_ref, sin_ref, gain_ref,
    keys_ref, down_out_ref, up_out_ref,
):
    total = jnp.zeros((8, 128), f32)
    acts = jnp.zeros((RANK, 128), f32)
    for j in range(8):
        part = got_ref[j, 128:].astype(f32)
        total += part[:8] + part[8:]
        acts += got_ref[j, :RANK].astype(f32)
    total = total[:1] * (adapter_scale * adapter_scale)
    move = adapter_scale * (step_length / jnp.sqrt(total + epsilon))
    down_out_ref[...] = at_ref[...] - move[:, :1] * down_ref[...]
    up = up_ref[...]
    up_out_ref[...] = b_ref[...] - move[:, :RANK] * jnp.concatenate([up[:, :RANK], up[:, RANK:]], axis=0)
    base = kept_ref[...].astype(f32) + came_ref[...].astype(f32)
    rank_act = base[512:] - move * acts
    for k in range(KV_HEADS):
        pair = []
        for j in (2 * k, 2 * k + 1):
            low = got_ref[j, 96:128].astype(f32) - move * got_ref[j, 64:96].astype(f32)
            pair.append(jnp.concatenate([low[:, :RANK], low[:, RANK:]], axis=0))
        up_new = jnp.concatenate(pair, axis=1).astype(bf16).astype(f32)
        head = base[128 * k : 128 * (k + 1)] + adapter_scale * dot(
            rank_act, up_new, (0, 0), lax.Precision.HIGHEST
        )
        mean = jnp.mean(head * head, axis=-1, keepdims=True)
        head = head * lax.rsqrt(mean + epsilon) * gain_ref[...]
        turned = head * cos_ref[...] + pltpu.roll(head, 64, 1) * sin_ref[...]
        keys_ref[:, :, 128 * k : 128 * (k + 1)] = turned.reshape(32, STEPS, 128).astype(bf16)


def finish(got, kept, came, down, up, at, b, cosine, sine, gain):
    return pl.pallas_call(
        finish_kernel,
        in_specs=[VMEM] * 10,
        out_specs=[VMEM] * 3,
        out_shape=(struct((32, STEPS, 512), bf16), struct((RANK, 512), f32), struct((RANK, RANK), f32)),
        compiler_params=SMALL,
        name="finish",
    )(got, kept, came, down, up, at, b, cosine, sine, gain)


def tables(positions):
    half = HEAD_DIM // 2
    index = jnp.arange(half, dtype=f32)
    freqs = jnp.exp(-jnp.log(f32(theta_base)) * 2.0 * index / HEAD_DIM)
    places = (positions[:, None] + jnp.arange(STEPS, dtype=jnp.int32)[None, :]).astype(f32)
    angle = places.reshape(-1, 1) * freqs[None, :]
    cosine = jnp.cos(angle)
    sine = jnp.sin(angle)
    return jnp.concatenate([cosine, cosine], axis=1), jnp.concatenate([-sine, sine], axis=1)


def on_device(x, c, a, b, w, hidden, positions, gain):
    at = a.T
    ct = c.T
    flat = hidden.reshape(1024, 512)

    i0, i1, i2 = (lax.axis_index(n) for n in ("t0", "t1", "t2"))

    got = lax.all_to_all(partials(x, ct, at, b), QUAD, 0, 0)
    mine = got.astype(f32).sum(axis=0).astype(bf16)
    mine, flat = lax.optimization_barrier((mine, flat))
    other = lax.ppermute(mine, "t2", SWAP)
    sent, kept = base_parts(i0.reshape(1), flat, w, at)
    other, sent, kept = lax.optimization_barrier((other, sent, kept))
    mine = (mine.astype(f32) + other.astype(f32)).astype(bf16)
    acts = lax.all_to_all(jnp.broadcast_to(mine, (4, 128, 512)), QUAD, 0, 0)

    grads = gradients(acts, x, ct)
    came = lax.ppermute(sent, "t0", SWAP)
    got = lax.all_to_all(grads, PLANE, 0, 0)

    def part(i):
        pick = lambda v: lax.dynamic_index_in_dim(v.reshape(2, 2, 576, 128), i, 0, keepdims=False)
        return pick(kept) + pick(came)

    sent1, kept1 = part(1 - i1), part(i1)
    came1 = lax.ppermute(sent1, "t1", SWAP)
    got, _ = lax.optimization_barrier((got, sent1))
    mine = got.astype(f32).sum(axis=0).astype(bf16)
    other = lax.ppermute(mine, "zh", SWAP)
    mine = (mine.astype(f32) + other.astype(f32)).astype(bf16)
    mine, came1 = lax.optimization_barrier((mine, came1))

    def half(i):
        pick = lambda v: lax.dynamic_index_in_dim(v, i, 0, keepdims=False)
        return pick(kept1) + pick(came1)

    send, sent2, kept2 = lax.optimization_barrier(
        (jnp.broadcast_to(mine, (32, 16, 128)), half(1 - i2), half(i2))
    )
    came2 = lax.ppermute(sent2, "t2", SWAP)
    got = lax.all_to_all(send, PLANE, 0, 0)

    send, down, up = rank_parts(got, flat, b)
    send, came2 = lax.optimization_barrier((send, came2))
    got = lax.all_to_all(send, TENSOR, 0, 0)
    cosine, sine = tables(positions)
    keys, new_down, new_up = finish(got, kept2, came2, down, up, at, b, cosine, sine, gain.reshape(1, 128))
    return keys, new_down.T, new_up


def solution(mesh):
    names = ("y", "x", "zh", "core") + TENSOR
    fine = Mesh(mesh.devices.reshape(4, 4, 2, 2, 2, 2, 2), names)
    in_specs = (
        P(DP, TENSOR),
        P(DP, TENSOR),
        P(TENSOR, None),
        P(None, TENSOR),
        P(TENSOR, None),
        P(DP, None, TENSOR),
        P(DP + TENSOR),
        P(),
    )
    out_specs = (P(DP + TENSOR, None, None), P(TENSOR, None), P(None, TENSOR))
    return jax.shard_map(on_device, mesh=fine, in_specs=in_specs, out_specs=out_specs, check_vma=False)
```

```python
import jax
import jax.numpy as jnp
from jax import lax
from jax.experimental import pallas as pl
from jax.experimental.pallas import tpu as pltpu
from jax.sharding import Mesh
from jax.sharding import PartitionSpec as P

HEAD_DIM = 128
KV_HEADS = 4
STEPS = 4
RANK = 64

adapter_scale = 2.0
step_length = 8.0
epsilon = 1e-06
theta_base = 1000000.0

TENSOR = ("t2", "t1", "t0")
QUAD = ("t1", "t0")
PLANE = ("y", "x", "core")
DP = ("y", "x", "zh", "core")
SWAP = [(0, 1), (1, 0)]
VMEM = pl.BlockSpec(memory_space=pltpu.VMEM)
SMALL = pltpu.CompilerParams(vmem_limit_bytes=6 * 1024 * 1024)
bf16 = jnp.bfloat16
f32 = jnp.float32


def dot(left, right, contract, precision=None):
    return lax.dot_general(
        left, right, ((contract[:1], contract[1:]), ((), ())),
        precision=precision, preferred_element_type=f32,
    )


def struct(shape, dtype):
    return jax.ShapeDtypeStruct(shape, dtype)


def partials_kernel(
    x_ref, ct_ref, at_ref, b_ref, out_ref, x_in, ct_in, at_in, b_in, sent, x_sems, sems, out_sems
):
    small = [
        pltpu.make_async_copy(source, target, sems.at[i])
        for i, (source, target) in enumerate(((at_ref, at_in), (b_ref, b_in), (ct_ref, ct_in)))
    ]
    large = [
        pltpu.make_async_copy(
            x_ref.at[pl.ds(512 * q, 512)], x_in.at[pl.ds(512 * q, 512)], x_sems.at[q]
        )
        for q in range(4)
    ]
    back = [pltpu.make_async_copy(sent.at[q], out_ref.at[q], out_sems.at[q]) for q in range(4)]
    for copy in small + large:
        copy.start()
    for copy in small:
        copy.wait()
    a = at_in[...].T.astype(bf16)
    b = b_in[...].astype(bf16)
    for q in range(4):
        sent[q, RANK:] = dot(b, ct_in[:, 512 * q : 512 * (q + 1)], (1, 0)).astype(bf16)
    for q in range(4):
        large[q].wait()
        sent[q, :RANK] = dot(x_in[512 * q : 512 * (q + 1)], a, (1, 0)).T.astype(bf16)
        back[q].start()
    for copy in back:
        copy.wait()


def partials(x, ct, at, b):
    return pl.pallas_call(
        partials_kernel,
        in_specs=[pl.BlockSpec(memory_space=pl.ANY)] * 4,
        out_specs=pl.BlockSpec(memory_space=pl.ANY),
        out_shape=struct((4, 2 * RANK, 512), bf16),
        scratch_shapes=[
            pltpu.VMEM((2048, 512), bf16),
            pltpu.VMEM((RANK, 2048), bf16),
            pltpu.VMEM((RANK, 512), f32),
            pltpu.VMEM((RANK, RANK), f32),
            pltpu.VMEM((4, 2 * RANK, 512), bf16),
            pltpu.SemaphoreType.DMA((4,)),
            pltpu.SemaphoreType.DMA((3,)),
            pltpu.SemaphoreType.DMA((4,)),
        ],
        name="partials",
    )(x, ct, at, b)


def base_kernel(me_ref, h_ref, w_ref, at_ref, send_ref, keep_ref):
    rows = h_ref[...]
    base = dot(rows, w_ref[...], (1, 0)).astype(bf16)
    acts = dot(rows, at_ref[...].T.astype(bf16), (1, 0)).T.astype(bf16)

    def write(out_ref):
        for k in range(KV_HEADS):
            out_ref[0, 128 * k : 128 * (k + 1)] = base[:, 128 * k : 128 * (k + 1)]
        out_ref[0, 512:] = acts

    @pl.when(pl.program_id(0) == 0)
    def _():
        write(send_ref)

    @pl.when(pl.program_id(0) == 1)
    def _():
        write(keep_ref)


def base_parts(me, flat, w, at):
    def rows(s, m, me_ref):
        t0 = jnp.where(s == 0, 1 - me_ref[0], me_ref[0])
        return (m % 2) * 4 + (m // 2) * 2 + t0, 0

    return pl.pallas_call(
        base_kernel,
        grid_spec=pltpu.PrefetchScalarGridSpec(
            num_scalar_prefetch=1,
            grid=(2, 4),
            in_specs=[
                pl.BlockSpec((128, 512), rows),
                pl.BlockSpec((512, 512), lambda s, m, me_ref: (0, 0)),
                pl.BlockSpec((RANK, 512), lambda s, m, me_ref: (0, 0)),
            ],
            out_specs=[
                pl.BlockSpec((1, 576, 128), lambda s, m, me_ref: (jnp.where(s == 0, m, 3), 0, 0)),
                pl.BlockSpec((1, 576, 128), lambda s, m, me_ref: (jnp.where(s == 0, 0, m), 0, 0)),
            ],
        ),
        out_shape=(struct((4, 576, 128), bf16), struct((4, 576, 128), bf16)),
        cost_estimate=pl.CostEstimate(flops=2 * 1024 * 512 * 576, bytes_accessed=3000000, transcendentals=0),
        compiler_params=SMALL,
        name="base",
    )(me, flat, w, at)


def grads_kernel(acts_ref, x_ref, ct_ref, out_ref):
    up = jnp.zeros((RANK, RANK), f32)
    for q in range(4):
        up += dot(acts_ref[q, :RANK], ct_ref[:, 512 * q : 512 * (q + 1)], (1, 1))
    folded = jnp.concatenate([up[:32], up[32:]], axis=1)
    down = jnp.zeros((RANK, 512), f32)
    for q in range(4):
        down += dot(acts_ref[q, RANK:], x_ref[512 * q : 512 * (q + 1)], (1, 0))
    for c in range(32):
        r, k = c // 4, c % 4
        tile = down[8 * r : 8 * r + 8, 128 * k : 128 * (k + 1)]
        row = jnp.broadcast_to(folded[c : c + 1], (8, 128))
        both = jnp.concatenate([tile, row], axis=0).astype(bf16)
        out_ref[c] = both


def gradients(acts, x, ct):
    return pl.pallas_call(
        grads_kernel,
        in_specs=[VMEM] * 3,
        out_specs=VMEM,
        out_shape=struct((32, 16, 128), bf16),
        compiler_params=SMALL,
        name="gradients",
    )(acts, x, ct)


def rank_kernel(got_ref, h_ref, b_ref, send_ref, down_ref, up_ref):
    for c in range(32):
        r, k = c // 4, c % 4
        both = got_ref[c].astype(f32)
        down_ref[8 * r : 8 * r + 8, 128 * k : 128 * (k + 1)] = both[:8]
        up_ref[c : c + 1] = both[8:9]
    down = down_ref[...]
    up = up_ref[...]
    square = jnp.sum(down * down) + jnp.sum(up * up)
    square = jnp.full((16, 128), square, f32)
    high = square.astype(bf16).astype(f32)
    first = lax.broadcasted_iota(jnp.int32, (16, 128), 0) < 8
    scalars = jnp.where(first, high, square - high).astype(bf16)
    low_b = b_ref[...].astype(bf16).astype(f32)
    small = jnp.concatenate(
        [up.astype(bf16), jnp.concatenate([low_b[:32], low_b[32:]], axis=1).astype(bf16), scalars],
        axis=0,
    )
    down = down.T.astype(bf16)
    for j in range(8):
        acts = dot(h_ref[128 * j : 128 * (j + 1)], down, (1, 0))
        send_ref[j, :RANK] = acts.T.astype(bf16)
        send_ref[j, RANK:] = small


def rank_parts(got, flat, b):
    return pl.pallas_call(
        rank_kernel,
        in_specs=[VMEM] * 3,
        out_specs=[VMEM] * 3,
        out_shape=(struct((8, 144, 128), bf16), struct((RANK, 512), f32), struct((32, 128), f32)),
        compiler_params=SMALL,
        name="rank",
    )(got, flat, b)


def finish_kernel(
    got_ref, kept_ref, came_ref, down_ref, up_ref, at_ref, b_ref, cos_ref, sin_ref, gain_ref,
    keys_ref, down_out_ref, up_out_ref,
):
    total = jnp.zeros((8, 128), f32)
    acts = jnp.zeros((RANK, 128), f32)
    for j in range(8):
        part = got_ref[j, 128:].astype(f32)
        total += part[:8] + part[8:]
        acts += got_ref[j, :RANK].astype(f32)
    total = total[:1] * (adapter_scale * adapter_scale)
    move = adapter_scale * (step_length / jnp.sqrt(total + epsilon))
    down_out_ref[...] = at_ref[...] - move[:, :1] * down_ref[...]
    up = up_ref[...]
    up_out_ref[...] = b_ref[...] - move[:, :RANK] * jnp.concatenate([up[:, :RANK], up[:, RANK:]], axis=0)
    base = kept_ref[...].astype(f32) + came_ref[...].astype(f32)
    rank_act = base[512:] - move * acts
    for k in range(KV_HEADS):
        pair = []
        for j in (2 * k, 2 * k + 1):
            low = got_ref[j, 96:128].astype(f32) - move * got_ref[j, 64:96].astype(f32)
            pair.append(jnp.concatenate([low[:, :RANK], low[:, RANK:]], axis=0))
        up_new = jnp.concatenate(pair, axis=1).astype(bf16).astype(f32)
        head = base[128 * k : 128 * (k + 1)] + adapter_scale * dot(
            rank_act, up_new, (0, 0), lax.Precision.HIGHEST
        )
        mean = jnp.mean(head * head, axis=-1, keepdims=True)
        head = head * lax.rsqrt(mean + epsilon) * gain_ref[...]
        turned = head * cos_ref[...] + pltpu.roll(head, 64, 1) * sin_ref[...]
        keys_ref[:, :, 128 * k : 128 * (k + 1)] = turned.reshape(32, STEPS, 128).astype(bf16)


def finish(got, kept, came, down, up, at, b, cosine, sine, gain):
    return pl.pallas_call(
        finish_kernel,
        in_specs=[VMEM] * 10,
        out_specs=[VMEM] * 3,
        out_shape=(struct((32, STEPS, 512), bf16), struct((RANK, 512), f32), struct((RANK, RANK), f32)),
        compiler_params=SMALL,
        name="finish",
    )(got, kept, came, down, up, at, b, cosine, sine, gain)


def tables(positions):
    half = HEAD_DIM // 2
    index = jnp.arange(half, dtype=f32)
    freqs = jnp.exp(-jnp.log(f32(theta_base)) * 2.0 * index / HEAD_DIM)
    places = (positions[:, None] + jnp.arange(STEPS, dtype=jnp.int32)[None, :]).astype(f32)
    angle = places.reshape(-1, 1) * freqs[None, :]
    cosine = jnp.cos(angle)
    sine = jnp.sin(angle)
    return jnp.concatenate([cosine, cosine], axis=1), jnp.concatenate([-sine, sine], axis=1)


def on_device(x, c, a, b, w, hidden, positions, gain):
    at = a.T
    ct = c.T
    flat = hidden.reshape(1024, 512)

    i0, i1, i2 = (lax.axis_index(n) for n in ("t0", "t1", "t2"))

    got = lax.all_to_all(partials(x, ct, at, b), QUAD, 0, 0)
    mine = got.astype(f32).sum(axis=0).astype(bf16)
    sent, kept = base_parts(i0.reshape(1), flat, w, at)
    mine, sent, kept = lax.optimization_barrier((mine, sent, kept))
    other = lax.ppermute(mine, "t2", SWAP)
    other, sent, kept = lax.optimization_barrier((other, sent, kept))
    mine = (mine.astype(f32) + other.astype(f32)).astype(bf16)
    acts = lax.all_to_all(jnp.broadcast_to(mine, (4, 128, 512)), QUAD, 0, 0)

    grads = gradients(acts, x, ct)
    came = lax.ppermute(sent, "t0", SWAP)
    got = lax.all_to_all(grads, PLANE, 0, 0)

    def part(i):
        pick = lambda v: lax.dynamic_index_in_dim(v.reshape(2, 2, 576, 128), i, 0, keepdims=False)
        return pick(kept) + pick(came)

    sent1, kept1 = part(1 - i1), part(i1)
    came1 = lax.ppermute(sent1, "t1", SWAP)
    got, _ = lax.optimization_barrier((got, sent1))
    mine = got.astype(f32).sum(axis=0).astype(bf16)
    other = lax.ppermute(mine, "zh", SWAP)
    mine = (mine.astype(f32) + other.astype(f32)).astype(bf16)
    mine, came1 = lax.optimization_barrier((mine, came1))

    def half(i):
        pick = lambda v: lax.dynamic_index_in_dim(v, i, 0, keepdims=False)
        return pick(kept1) + pick(came1)

    send, sent2, kept2 = lax.optimization_barrier(
        (jnp.broadcast_to(mine, (32, 16, 128)), half(1 - i2), half(i2))
    )
    came2 = lax.ppermute(sent2, "t2", SWAP)
    got = lax.all_to_all(send, PLANE, 0, 0)

    send, down, up = rank_parts(got, flat, b)
    send, came2 = lax.optimization_barrier((send, came2))
    got = lax.all_to_all(send, TENSOR, 0, 0)
    cosine, sine = tables(positions)
    keys, new_down, new_up = finish(got, kept2, came2, down, up, at, b, cosine, sine, gain.reshape(1, 128))
    return keys, new_down.T, new_up


def solution(mesh):
    names = ("y", "x", "zh", "core") + TENSOR
    fine = Mesh(mesh.devices.reshape(4, 4, 2, 2, 2, 2, 2), names)
    in_specs = (
        P(DP, TENSOR),
        P(DP, TENSOR),
        P(TENSOR, None),
        P(None, TENSOR),
        P(TENSOR, None),
        P(DP, None, TENSOR),
        P(DP + TENSOR),
        P(),
    )
    out_specs = (P(DP + TENSOR, None, None), P(TENSOR, None), P(None, TENSOR))
    return jax.shard_map(on_device, mesh=fine, in_specs=in_specs, out_specs=out_specs, check_vma=False)
```
